32 devices in a mesh: groups: 2 (over x), fsdp: 16 (over z, y, core).
Axes of the slice: x: 2, y: 2, z: 4, core: 2. Of those that a mesh axis runs over, the one named last changes fastest.
Arguments:
- tokens: bfloat16 [4096, 8192], P(('groups', 'fsdp')), parts along dimension 0, may hold values from -6 to 6
- token_job_index: int32 [4096, 1], P(('groups', 'fsdp')), parts along dimension 0, may hold values from 0 to 15; in each aligned block of 128 rows (0 to 127, 128 to 255, ...) at most 10 rows name the same one
- frozen_value_weight: bfloat16 [8192, 1024], P('fsdp'), may hold values from -0.0625 to 0.0625
- output_gradient: bfloat16 [4096, 1024], P(('groups', 'fsdp')), parts along dimension 0, may hold values from -6 to 6
- down_factor: bfloat16 [32, 8192, 64], P(('groups', 'fsdp')), parts along dimension 0, may hold values from -0.0625 to 0.0625
- up_factor: bfloat16 [32, 64, 1024], P(('groups', 'fsdp')), parts along dimension 0, may hold values from -0.75 to 0.75
- job_adapter_rank: int32 [32], P(('groups', 'fsdp')), parts along dimension 0, may hold values from 16 to 64, as said below
Outputs:
- values: bfloat16 [4096, 1024], P(('groups', 'fsdp')), parts along dimension 0
- grad_in: bfloat16 [4096, 8192], P(('groups', 'fsdp')), parts along dimension 0
- down_gradient: float32 [32, 8192, 64], P(('groups', 'fsdp')), parts along dimension 0
- up_gradient: float32 [32, 64, 1024], P(('groups', 'fsdp')), parts along dimension 0
The draws below stay inside these ranges and needn't reach their ends.
There are 2 independent parts, one for each index of `groups`. The reference program is written for one: setup_inputs(seed, part) draws one part's arguments, and reference() takes and returns one part's arrays. A program takes and returns all parts, laid end to end along the dimension named above; an argument that names none is the same for every part. Nothing has to cross between parts.
Inputs may be any that keep to these rules, and one draw needn't show every extreme that they name: `token_job_index`: among the 128 tokens of one device at most 10 belong to one job, and every job has tokens somewhere in the group. `job_adapter_rank`: ranks are multiples of 16.
All inputs are finite; a program needn't handle non-finite values.
Results may differ from the reference program's by a relative error of at most 0.0044.
Values may be sent and summed in bfloat16 or wider, within the bound.
A program may use at most 128 MiB of HBM per device.

```python
import math
import jax
import jax.numpy as jnp
import numpy as np
from jax import lax

MODEL_WIDTH = 8192
VALUE_WIDTH = 1024
MAXIMUM_RANK = 64
TOK_DEV = 128
ADAPTER_JOBS = 16
CAP = 10
TOKENS = 2048
N_FSDP = 16


def draw_job_adapter_rank(key, part):
    key = jax.random.fold_in(key, 7)
    order = jax.random.permutation(key, ADAPTER_JOBS)
    return (16 * (1 + order % (MAXIMUM_RANK // 16))).astype(jnp.int32)


def shard_levels(own_key, extent, cuts, least, largest):
    factor_of = 1.0
    for dim, parts in cuts:
        heights = jax.random.uniform(jax.random.fold_in(jax.random.fold_in(own_key, 6), dim), (parts,), jnp.float32, least / len(cuts), largest / len(cuts))
        factor_of = factor_of * jnp.repeat(jnp.exp(heights), extent[dim] // parts).reshape((-1,) + (1,) * (len(extent) - 1 - dim))
    return factor_of


def deal_out(key, own, number, rows, number_of, top, most, slope):
    order = jax.random.permutation(key, number_of)
    heavy_load, usual = shares(number_of, rows * top, most, slope, True), shares(number_of, rows * top, most, slope, False)
    places = jnp.arange(number_of)

    def named(tallies, offset_by):
        used = int((tallies > 0).sum())
        fixed = max(1, used // 4)
        moved = fixed + (places - fixed + offset_by * (used - fixed)) % max(1, number_of - fixed)
        return jnp.zeros((number_of,), jnp.int32).at[order[jnp.where(places < fixed, places, moved)]].set(jnp.asarray(tallies, jnp.int32))

    tallies = jnp.where(number % 4 == 0, named(heavy_load, number // 4), named(usual, number - number // 4 - 1))
    mixed = jax.random.permutation(jax.random.fold_in(own, 3), number_of)
    giver, taker = mixed[0:number_of // 2 * 2:2], mixed[1:number_of // 2 * 2:2]
    margin = jnp.minimum(tallies[giver] - 1, most - tallies[taker]) // 2
    margin = jnp.where((giver == order[0]) | (taker == order[0]) | (tallies[taker] == 0), 0, jnp.maximum(margin, 0))
    moved = jax.random.randint(jax.random.fold_in(own, 4), (number_of // 2,), 0, 1 << 20) % (margin + 1)
    tallies = tallies.at[giver].add(-moved).at[taker].add(moved)
    labels = jnp.searchsorted(jnp.cumsum(tallies), jnp.arange(rows * top), side="right").astype(jnp.int32)
    listing = labels.reshape(top, rows).T
    listing = listing[jax.random.permutation(jax.random.fold_in(own, 1), rows)]
    offset_by = jax.random.randint(jax.random.fold_in(own, 2), (rows, 1), 0, top)
    return jnp.take_along_axis(listing, (jnp.arange(top)[None, :] + offset_by) % top, axis=1)


def shares(number_of, total, bound, lean, full):
    weights = [(1 << 20) // math.isqrt(grade ** lean) + 1 for grade in range(1, number_of + 1)]
    largest = bound if full else min(bound, max(-(-total // number_of), total * weights[0] // sum(weights)))
    least = 1 if total - largest >= number_of - 1 else 0
    given, surplus = [largest] + [least] * (number_of - 1), total - largest - least * (number_of - 1)
    while surplus > 0:
        movable = [i for i in range(1, number_of) if given[i] < largest] or [i for i in range(1, number_of) if given[i] < bound]
        whole, budget = sum([weights[i] for i in movable]), surplus
        for i in movable:
            extra = min(bound - given[i], max(1, budget * weights[i] // whole), surplus)
            given[i] = given[i] + extra
            surplus = surplus - extra
    return np.array(given)


def normal_values(key, dims, deviation, bound, pieces=(), kind=jnp.bfloat16):
    factor_of = shard_levels(key, dims, pieces, -0.22, 0.18) if pieces else 1.0
    array = jax.random.normal(key, dims, jnp.float32) * deviation * factor_of
    return jnp.minimum(jnp.maximum(array, -bound), bound).astype(kind)


def setup_inputs(seed: int = 0, part: int = 0) -> dict:
    key_of = jax.random.split(jax.random.key(seed), 8)
    part_splits = jax.random.split(jax.random.fold_in(key_of[7], part), 8)
    tokens = normal_values(part_splits[0], (TOKENS, MODEL_WIDTH), 1.0, 6.0, ((0, 16),))
    token_job_index_keys = jax.random.split(jax.random.fold_in(part_splits[1], 1), TOKENS // TOK_DEV)
    token_job_index_turns = jax.random.permutation(jax.random.fold_in(part_splits[1], 3), TOKENS // TOK_DEV)
    token_job_index = jax.vmap(lambda own, number: deal_out(jax.random.fold_in(part_splits[1], 2), own, number, TOK_DEV, ADAPTER_JOBS, 1, CAP, 2))(token_job_index_keys, token_job_index_turns).reshape((TOKENS, 1))
    frozen_value_weight = normal_values(key_of[2], (MODEL_WIDTH, VALUE_WIDTH), MODEL_WIDTH ** -0.5, 0.0625, ((0, 16),))
    output_gradient = normal_values(part_splits[3], (TOKENS, VALUE_WIDTH), 1.0, 6.0, ((0, 16),))
    down_factor = normal_values(part_splits[4], (ADAPTER_JOBS, MODEL_WIDTH, MAXIMUM_RANK), MODEL_WIDTH ** -0.5, 0.0625, ((0, 16),))
    up_factor = normal_values(part_splits[5], (ADAPTER_JOBS, MAXIMUM_RANK, VALUE_WIDTH), MAXIMUM_RANK ** -0.5, 0.75, ((0, 16),))
    job_adapter_rank = draw_job_adapter_rank(jax.random.fold_in(jax.random.fold_in(key_of[7], part), 71), part)
    return dict(tokens=tokens, token_job_index=token_job_index, frozen_value_weight=frozen_value_weight, output_gradient=output_gradient, down_factor=down_factor, up_factor=up_factor, job_adapter_rank=job_adapter_rank)


def reference(tokens, token_job_index, frozen_value_weight, output_gradient, down_factor, up_factor, job_adapter_rank):
    group_size = N_FSDP
    job_ids = token_job_index[:, 0].astype(jnp.int32)
    onehot = (job_ids[:, None] == jnp.arange(ADAPTER_JOBS, dtype=jnp.int32)[None, :]).astype(jnp.int32)
    per_device = onehot.reshape(group_size, TOK_DEV, ADAPTER_JOBS)
    before = jnp.cumsum(per_device, axis=1) - per_device
    position = jnp.sum(before * per_device, axis=2).reshape(TOKENS).astype(jnp.int32)
    device_of = (jnp.arange(TOKENS, dtype=jnp.int32) // TOK_DEV).astype(jnp.int32)
    flat_slot = ((job_ids * group_size + device_of) * CAP + position).astype(jnp.int32)
    position_lookup = jnp.full((ADAPTER_JOBS * group_size * CAP,), TOKENS, jnp.int32)
    position_lookup = position_lookup.at[flat_slot].set(jnp.arange(TOKENS, dtype=jnp.int32))
    position_lookup = position_lookup.reshape(ADAPTER_JOBS, group_size * CAP)
    padded_x = jnp.concatenate([tokens, jnp.zeros((1, MODEL_WIDTH), tokens.dtype)], axis=0)
    padded_g = jnp.concatenate([output_gradient, jnp.zeros((1, VALUE_WIDTH), output_gradient.dtype)], axis=0)

    def single_job_fn(packed):
        row_index, down_matrix, up_matrix, adapter_rank_value = packed
        dispatched_input = padded_x[row_index]
        dispatched_gradient = padded_g[row_index]
        adapter_rank_mask = (jnp.arange(MAXIMUM_RANK) < adapter_rank_value).astype(jnp.float32)
        adapter_scale = 32.0 / adapter_rank_value.astype(jnp.float32)
        narrow_product = (jnp.dot(dispatched_input, down_matrix, preferred_element_type=jnp.float32) * adapter_rank_mask).astype(jnp.bfloat16)
        adapter_output = (jnp.dot(narrow_product, up_matrix, preferred_element_type=jnp.float32) * adapter_scale).astype(jnp.bfloat16)
        narrow_gradient = (jnp.dot(dispatched_gradient, up_matrix.T, preferred_element_type=jnp.float32) * (adapter_scale * adapter_rank_mask)).astype(jnp.bfloat16)
        up_gradient = jnp.dot(narrow_product.T, dispatched_gradient, preferred_element_type=jnp.float32) * adapter_scale
        down_gradient = jnp.dot(dispatched_input.T, narrow_gradient, preferred_element_type=jnp.float32)
        adapter_backward = jnp.dot(narrow_gradient, down_matrix.T, preferred_element_type=jnp.float32).astype(jnp.bfloat16)
        return adapter_output, adapter_backward, down_gradient, up_gradient

    gathered_output, gathered_backward, down_gradient, up_gradient = lax.map(single_job_fn, (position_lookup, down_factor, up_factor, job_adapter_rank))
    out_tok = gathered_output.reshape(ADAPTER_JOBS * group_size * CAP, VALUE_WIDTH)[flat_slot]
    back_tok = gathered_backward.reshape(ADAPTER_JOBS * group_size * CAP, MODEL_WIDTH)[flat_slot]
    values = (jnp.dot(tokens, frozen_value_weight, preferred_element_type=jnp.float32) + out_tok.astype(jnp.float32)).astype(jnp.bfloat16)
    grad_in = (jnp.dot(output_gradient, frozen_value_weight.T, preferred_element_type=jnp.float32) + back_tok.astype(jnp.float32)).astype(jnp.bfloat16)
    return values, grad_in, down_gradient, up_gradient
```

```python
import functools

import jax
import jax.numpy as jnp
import numpy as np
from jax import lax
from jax.experimental import pallas as pl
from jax.experimental.pallas import tpu as pltpu
from jax.sharding import PartitionSpec as P

CHUNKS = 8
PIECES = 2
BF16 = jnp.bfloat16
F32 = jnp.float32
MESH = pl.DeviceIdType.MESH


def dot(a, b, ca=1, cb=0):
    return lax.dot_general(a, b, (((ca,), (cb,)), ((), ())), preferred_element_type=F32)


def kernel(
    n,
    cap,
    rank_ref,
    jobc_ref,
    jobr_ref,
    keyc_ref,
    keyr_ref,
    foldc_ref,
    foldr_ref,
    chunk_ref,
    tok_ref,
    g_ref,
    w_ref,
    a_ref,
    up_ref,
    val_ref,
    gin_ref,
    da_ref,
    du_ref,
    wbuf,
    stack,
    send,
    recv,
    ret,
    back,
    acat,
    upst,
    lowx,
    lgx,
    gacc,
    vacc,
    wl_sem,
    w_send,
    w_recv,
    s_send,
    s_recv,
    r_send,
    r_recv,
):
    me = lax.axis_index("fsdp")
    rb = CHUNKS * cap
    gb = 4 * rb
    outer = n // 4
    slots = n * cap
    tl, width = tok_ref.shape
    wide = g_ref.shape[1]
    xw = width // CHUNKS
    gw = wide // CHUNKS
    rank_max = up_ref.shape[0]
    lanes = CHUNKS * rank_max
    rows = wbuf.shape[1]
    prow = rows // PIECES
    o, m, c = me // 4, lax.rem(me // 2, 2), lax.rem(me, 2)

    def idx(oo, mm, cc):
        return (oo * 2 + mm) * 2 + cc

    local = pltpu.make_async_copy(w_ref, wbuf.at[me], wl_sem)
    local.start()

    barrier = pltpu.get_barrier_semaphore()

    @pl.loop(1, n)
    def _(d):
        pl.semaphore_signal(
            barrier, inc=1, device_id={"fsdp": lax.rem(me + d, n)}, device_id_type=MESH
        )

    pl.semaphore_wait(barrier, n - 1)
    local.wait()

    def w_copy(shard, piece, kind, dest):
        part = wbuf.at[shard, pl.ds(piece * prow, prow)]
        return pltpu.make_async_remote_copy(
            src_ref=part,
            dst_ref=part,
            send_sem=w_send.at[kind, shard, piece],
            recv_sem=w_recv.at[shard, piece],
            device_id={"fsdp": dest},
            device_id_type=MESH,
        )

    def up_dest():
        return lax.rem(me + 4, n)

    def down_dest():
        return lax.rem(me + n - 4, n)

    mid = idx(o, 1 - m, c)
    core = idx(o, m, 1 - c)

    for p in range(PIECES):

        @pl.when(o + 1 < outer)
        def _():
            w_copy(me, p, 0, up_dest()).start()

        @pl.when(o > 0)
        def _():
            w_copy(me, p, 1, down_dest()).start()

    jc = jobc_ref[...]
    jr = jobr_ref[...]
    same = jc == jr
    ri = lax.broadcasted_iota(jnp.int32, (tl, tl), 0)
    ci = lax.broadcasted_iota(jnp.int32, (tl, tl), 1)
    one = jnp.where(same, 1.0, 0.0)
    pos_c = jnp.sum(jnp.where(ci < ri, one, 0.0), axis=1, keepdims=True).astype(jnp.int32)
    pos_r = jnp.sum(jnp.where(ri < ci, one, 0.0), axis=0, keepdims=True).astype(jnp.int32)
    slot_c = jc * cap + pos_c
    slot_r = jr * cap + pos_r

    for k in range(CHUNKS):
        stack[k * tl : (k + 1) * tl, :xw] = tok_ref[:, k * xw : (k + 1) * xw]
        stack[k * tl : (k + 1) * tl, xw:] = g_ref[:, k * gw : (k + 1) * gw]
    tok_key = jnp.concatenate([slot_r + k * slots for k in range(CHUNKS)], axis=1)

    def s_copy(j, k):
        return pltpu.make_async_remote_copy(
            src_ref=send.at[pl.ds(j * rb, rb)],
            dst_ref=recv.at[pl.ds(k * rb, rb)],
            send_sem=s_send.at[j],
            recv_sem=s_recv.at[k],
            device_id={"fsdp": j},
            device_id_type=MESH,
        )

    def r_copy(j, k):
        return pltpu.make_async_remote_copy(
            src_ref=ret.at[pl.ds(j * rb, rb)],
            dst_ref=back.at[pl.ds(k * rb, rb)],
            send_sem=r_send.at[j],
            recv_sem=r_recv.at[k],
            device_id={"fsdp": j},
            device_id_type=MESH,
        )

    def quad(i):
        return lax.rem(o + i, outer)

    @pl.loop(1, outer + 1)
    def _(i):
        q = quad(i)
        key = keyc_ref[...] + q * (4 * cap)
        sel = jnp.where(key == tok_key, 1.0, 0.0).astype(BF16)
        send[pl.ds(q * gb, gb), :] = dot(sel, stack[...]).astype(BF16)
        for e in range(4):
            j = q * 4 + e

            @pl.when(j != me)
            def _():
                s_copy(j, me).start()

            @pl.when(j == me)
            def _():
                recv[pl.ds(me * rb, rb), :] = send[pl.ds(me * rb, rb), :]

    for p in range(PIECES):
        w_copy(me, p, 2, mid).start()
        w_copy(me, p, 3, core).start()

    for k in range(CHUNKS):
        acat[:, k * rank_max : (k + 1) * rank_max] = a_ref[k * xw : (k + 1) * xw, :]
        upst[k * rank_max : (k + 1) * rank_max, :] = up_ref[:, k * gw : (k + 1) * gw]

    @pl.loop(1, outer)
    def _(s):
        for p in range(PIECES):

            @pl.when(o - s >= 0)
            def _():
                k = idx(o - s, m, c)
                w_copy(k, p, 0, me).wait_recv()

                @pl.when(o + 1 < outer)
                def _():
                    w_copy(k, p, 0, up_dest()).start()

                w_copy(k, p, 2, mid).start()
                w_copy(k, p, 3, core).start()

            @pl.when(o + s < outer)
            def _():
                k = idx(o + s, m, c)
                w_copy(k, p, 1, me).wait_recv()

                @pl.when(o > 0)
                def _():
                    w_copy(k, p, 1, down_dest()).start()

                w_copy(k, p, 2, mid).start()
                w_copy(k, p, 3, core).start()

    rank = rank_ref[0]
    scale = 32.0 / jnp.full((1, 128), rank, jnp.int32).astype(F32)
    lane = lax.broadcasted_iota(jnp.int32, (1, 128), 1)
    mask = jnp.where(lax.rem(lane, rank_max) < rank, 1.0, 0.0)
    lane_chunk = lax.broadcasted_iota(jnp.int32, (gb, lanes), 1) // rank_max
    diag = lane_chunk == chunk_ref[...]
    fold = jnp.where(foldc_ref[...] == foldr_ref[...], 1.0, 0.0).astype(BF16)
    half = lax.broadcasted_iota(jnp.int32, (gb, 128), 1) < rank_max

    def narrow(y):
        y = jnp.where(diag, y, 0.0)
        z = y[:, :128]
        for k in range(1, lanes // 128):
            z = z + y[:, k * 128 : (k + 1) * 128]
        z = z + pltpu.roll(z, rank_max, 1)
        hi = z.astype(BF16).astype(F32)
        return jnp.where(half, hi, z - hi).astype(BF16)

    def widen(z):
        return jnp.where(diag, jnp.concatenate([z] * (lanes // 128), axis=1), 0.0).astype(BF16)

    @pl.loop(0, outer)
    def _(i):
        q = lax.rem(o + outer - i, outer)
        for e in range(4):
            j = q * 4 + e

            @pl.when(j != me)
            def _():
                s_copy(j, j).wait_recv()

        at = pl.ds(q * gb, gb)
        low = narrow(dot(recv[at, :xw], acat[...]))
        lg = narrow(dot(recv[at, xw:], upst[...], 1, 1))
        both = dot(fold, jnp.concatenate([low, lg], axis=1))
        low = both[:, :128]
        lg = both[:, 128:]
        low = ((low + pltpu.roll(low, rank_max, 1)) * mask).astype(BF16).astype(F32)
        lg = ((lg + pltpu.roll(lg, rank_max, 1)) * (scale * mask)).astype(BF16).astype(F32)
        low = widen(low)
        lg = widen(lg)
        lowx[at, :] = low
        lgx[at, :] = lg
        ret[at, :xw] = dot(lg, acat[...], 1, 1).astype(BF16)
        ret[at, xw:] = (dot(low, upst[...]) * scale[:, :1]).astype(BF16)
        for e in range(4):
            j = q * 4 + e

            @pl.when(j != me)
            def _():
                r_copy(j, me).start()

            @pl.when(j == me)
            def _():
                back[pl.ds(me * rb, rb), :] = ret[pl.ds(me * rb, rb), :]

    du = dot(lowx[...], recv[:, xw:], 0, 0) * scale[:, :1]
    for k in range(CHUNKS):
        du_ref[:, k * gw : (k + 1) * gw] = du[k * rank_max : (k + 1) * rank_max, :]

    for k in range(xw // 256):
        da = dot(recv[:, k * 256 : (k + 1) * 256], lgx[...], 0, 0)
        for e in range(CHUNKS):
            da_ref[pl.ds(e * xw + k * 256, 256), :] = da[:, e * rank_max : (e + 1) * rank_max]

    @pl.loop(0, outer)
    def _(s):
        for p in range(PIECES):

            @pl.when(o - s >= 0)
            def _():
                k = idx(o - s, 1 - m, c)
                w_copy(k, p, 2, me).wait_recv()
                w_copy(k, p, 3, core).start()

            @pl.when((s > 0) & (o + s < outer))
            def _():
                k = idx(o + s, 1 - m, c)
                w_copy(k, p, 2, me).wait_recv()
                w_copy(k, p, 3, core).start()

    vacc[...] = jnp.zeros_like(vacc)

    def product(k):
        cols = pl.ds(pl.multiple_of(k * rows, rows), rows)
        vacc[...] += dot(tok_ref[:, cols], wbuf[k])
        gacc[:, cols] = dot(g_ref[...], wbuf[k], 1, 1)

    @pl.loop(0, n // 2)
    def _(k):
        product(2 * k + c)

    @pl.loop(0, n // 2)
    def _(k):
        s = 2 * k + 1 - c
        for p in range(PIECES):
            w_copy(s, p, 3, me).wait_recv()
        product(s)

    @pl.loop(0, n)
    def _(j):
        @pl.when(j != me)
        def _():
            r_copy(j, j).wait_recv()

    vsum = jnp.zeros((tl, wide), F32)
    parts = []
    for k in range(CHUNKS):
        sel = jnp.where(slot_c + k * slots == keyr_ref[...], 1.0, 0.0).astype(BF16)
        add = dot(sel, back[...])
        cols = slice(k * xw, (k + 1) * xw)
        gin_ref[:, cols] = (gacc[:, cols] + add[:, :xw]).astype(BF16)
        vcols = slice(k * gw, (k + 1) * gw)
        val_ref[:, vcols] = (vacc[:, vcols] + add[:, xw:]).astype(BF16)

    @pl.loop(0, n)
    def _(j):
        @pl.when(j != me)
        def _():
            s_copy(j, me).wait_send()
            r_copy(j, me).wait_send()

    @pl.loop(0, outer)
    def _(z):
        for p in range(PIECES):
            k = idx(z, m, c)

            @pl.when((z <= o) & (o + 1 < outer))
            def _():
                w_copy(k, p, 0, up_dest()).wait_send()

            @pl.when((z >= o) & (o > 0))
            def _():
                w_copy(k, p, 1, down_dest()).wait_send()

            w_copy(k, p, 2, mid).wait_send()
            w_copy(k, p, 3, core).wait_send()
            w_copy(idx(z, 1 - m, c), p, 3, core).wait_send()


def shards(tokens, job, weight, gradient, down, up, rank):
    n = lax.axis_size("fsdp")
    tl, width = tokens.shape
    wide = gradient.shape[1]
    rank_max = up.shape[1]
    cap = 5 * tl // (4 * n)
    rb = CHUNKS * cap
    gb = 4 * rb
    total = n * rb
    xw, gw = width // CHUNKS, wide // CHUNKS
    lanes = CHUNKS * rank_max

    i = np.arange(total)
    key = (i % rb // cap) * (n * cap) + (i // rb) * cap + i % cap
    fold = (i // rb) * cap + i % cap
    consts = [
        key[:gb, None],
        key[None, :],
        fold[:gb, None],
        fold[None, :gb],
        (i % rb // cap)[:gb, None],
    ]
    consts = [jnp.asarray(v, jnp.int32) for v in consts]

    vmem = pl.BlockSpec(memory_space=pltpu.VMEM)
    args = (rank, job, job.reshape(1, tl), *consts, tokens, gradient, weight, down[0], up[0])
    specs = [pl.BlockSpec(memory_space=pltpu.SMEM)] + [vmem] * 9
    specs += [pl.BlockSpec(memory_space=pl.ANY)] + [vmem] * 2
    dma = pltpu.SemaphoreType.DMA
    values, grad_in, d_down, d_up = pl.pallas_call(
        functools.partial(kernel, n, cap),
        out_shape=(
            jax.ShapeDtypeStruct((tl, wide), BF16),
            jax.ShapeDtypeStruct((tl, width), BF16),
            jax.ShapeDtypeStruct((width, rank_max), F32),
            jax.ShapeDtypeStruct((rank_max, wide), F32),
        ),
        in_specs=specs,
        out_specs=(vmem,) * 4,
        scratch_shapes=[
            pltpu.VMEM((n, *weight.shape), BF16),
            pltpu.VMEM((CHUNKS * tl, xw + gw), BF16),
            pltpu.VMEM((total, xw + gw), BF16),
            pltpu.VMEM((total, xw + gw), BF16),
            pltpu.VMEM((total, xw + gw), BF16),
            pltpu.VMEM((total, xw + gw), BF16),
            pltpu.VMEM((xw, lanes), BF16),
            pltpu.VMEM((lanes, gw), BF16),
            pltpu.VMEM((total, lanes), BF16),
            pltpu.VMEM((total, lanes), BF16),
            pltpu.VMEM((tl, width), F32),
            pltpu.VMEM((tl, wide), F32),
            dma,
            dma((4, n, PIECES)),
            dma((n, PIECES)),
            dma((n,)),
            dma((n,)),
            dma((n,)),
            dma((n,)),
        ],
        compiler_params=pltpu.CompilerParams(
            collective_id=0, has_side_effects=True, vmem_limit_bytes=62 * 1024 * 1024
        ),
        cost_estimate=pl.CostEstimate(
            flops=16 * 10**9, bytes_accessed=16 * 2**20, transcendentals=0
        ),
    )(*args)
    return values, grad_in, d_down[None], d_up[None]


def solution(mesh):
    rows = P(("groups", "fsdp"), None)
    jobs = P(("groups", "fsdp"), None, None)
    return jax.shard_map(
        shards,
        mesh=mesh,
        in_specs=(rows, rows, P("fsdp", None), rows, jobs, jobs, P(("groups", "fsdp"))),
        out_specs=(rows, rows, jobs, jobs),
        check_vma=False,
    )
```

```python
import functools

import jax
import jax.numpy as jnp
import numpy as np
from jax import lax
from jax.experimental import pallas as pl
from jax.experimental.pallas import tpu as pltpu
from jax.sharding import PartitionSpec as P

CHUNKS = 8
PIECES = 2
BF16 = jnp.bfloat16
F32 = jnp.float32
MESH = pl.DeviceIdType.MESH


def dot(a, b, ca=1, cb=0):
    return lax.dot_general(a, b, (((ca,), (cb,)), ((), ())), preferred_element_type=F32)


def kernel(
    n,
    cap,
    rank_ref,
    jobc_ref,
    jobr_ref,
    keyc_ref,
    keyr_ref,
    foldc_ref,
    foldr_ref,
    chunk_ref,
    tok_ref,
    g_ref,
    w_ref,
    a_ref,
    up_ref,
    val_ref,
    gin_ref,
    da_ref,
    du_ref,
    wbuf,
    stack,
    send,
    recv,
    ret,
    back,
    acat,
    upst,
    lowx,
    lgx,
    gacc,
    vacc,
    wl_sem,
    w_send,
    w_recv,
    s_send,
    s_recv,
    r_send,
    r_recv,
):
    me = lax.axis_index("fsdp")
    rb = CHUNKS * cap
    gb = 4 * rb
    outer = n // 4
    slots = n * cap
    tl, width = tok_ref.shape
    wide = g_ref.shape[1]
    xw = width // CHUNKS
    gw = wide // CHUNKS
    rank_max = up_ref.shape[0]
    lanes = CHUNKS * rank_max
    rows = wbuf.shape[1]
    prow = rows // PIECES
    o, m, c = me // 4, lax.rem(me // 2, 2), lax.rem(me, 2)

    def idx(oo, mm, cc):
        return (oo * 2 + mm) * 2 + cc

    local = pltpu.make_async_copy(w_ref, wbuf.at[me], wl_sem)
    local.start()

    barrier = pltpu.get_barrier_semaphore()

    @pl.loop(1, n)
    def _(d):
        pl.semaphore_signal(
            barrier, inc=1, device_id={"fsdp": lax.rem(me + d, n)}, device_id_type=MESH
        )

    pair = lax.axis_size("groups") % 2 == 0
    group = lax.axis_index("groups")
    other = group + 1 - 2 * lax.rem(group, 2) if pair else group
    mine = [lax.rem(group, 2)] if pair else list(range(PIECES))
    theirs = [1 - lax.rem(group, 2)] if pair else []

    if pair:
        pl.semaphore_signal(
            barrier, inc=1, device_id={"groups": other, "fsdp": me}, device_id_type=MESH
        )
    pl.semaphore_wait(barrier, n if pair else n - 1)
    local.wait()

    def w_copy(shard, piece, kind, dest):
        part = wbuf.at[shard, pl.ds(pl.multiple_of(piece * prow, prow), prow)]
        return pltpu.make_async_remote_copy(
            src_ref=part,
            dst_ref=part,
            send_sem=w_send.at[kind, shard, piece],
            recv_sem=w_recv.at[shard, piece],
            device_id={"groups": other if kind == 4 else group, "fsdp": dest},
            device_id_type=MESH,
        )

    def up_dest():
        return lax.rem(me + 4, n)

    def down_dest():
        return lax.rem(me + n - 4, n)

    mid = idx(o, 1 - m, c)
    core = idx(o, m, 1 - c)

    for p in mine:

        @pl.when(o + 1 < outer)
        def _():
            w_copy(me, p, 0, up_dest()).start()

        @pl.when(o > 0)
        def _():
            w_copy(me, p, 1, down_dest()).start()

    for p in mine:
        w_copy(me, p, 2, mid).start()
    for p in range(PIECES):
        w_copy(me, p, 3, core).start()

    jc = jobc_ref[...]
    jr = jobr_ref[...]
    same = jc == jr
    ri = lax.broadcasted_iota(jnp.int32, (tl, tl), 0)
    ci = lax.broadcasted_iota(jnp.int32, (tl, tl), 1)
    one = jnp.where(same, 1.0, 0.0)
    pos_c = jnp.sum(jnp.where(ci < ri, one, 0.0), axis=1, keepdims=True).astype(jnp.int32)
    pos_r = jnp.sum(jnp.where(ri < ci, one, 0.0), axis=0, keepdims=True).astype(jnp.int32)
    slot_c = jc * cap + pos_c
    slot_r = jr * cap + pos_r

    for k in range(CHUNKS):
        stack[k * tl : (k + 1) * tl, :xw] = tok_ref[:, k * xw : (k + 1) * xw]
        stack[k * tl : (k + 1) * tl, xw:] = g_ref[:, k * gw : (k + 1) * gw]
    tok_key = jnp.concatenate([slot_r + k * slots for k in range(CHUNKS)], axis=1)

    def s_copy(j, k):
        return pltpu.make_async_remote_copy(
            src_ref=send.at[pl.ds(j * rb, rb)],
            dst_ref=recv.at[pl.ds(k * rb, rb)],
            send_sem=s_send.at[j],
            recv_sem=s_recv.at[k],
            device_id={"fsdp": j},
            device_id_type=MESH,
        )

    def r_copy(j, k):
        return pltpu.make_async_remote_copy(
            src_ref=ret.at[pl.ds(j * rb, rb)],
            dst_ref=back.at[pl.ds(k * rb, rb)],
            send_sem=r_send.at[j],
            recv_sem=r_recv.at[k],
            device_id={"fsdp": j},
            device_id_type=MESH,
        )

    def quad(i):
        return lax.rem(o + i, outer)

    @pl.loop(1, outer + 1)
    def _(i):
        q = quad(i)
        key = keyc_ref[...] + q * (4 * cap)
        sel = jnp.where(key == tok_key, 1.0, 0.0).astype(BF16)
        send[pl.ds(q * gb, gb), :] = dot(sel, stack[...]).astype(BF16)

    for k in range(CHUNKS):
        acat[k * rank_max : (k + 1) * rank_max, :] = a_ref[:, k * xw : (k + 1) * xw]
        upst[k * rank_max : (k + 1) * rank_max, :] = up_ref[:, k * gw : (k + 1) * gw]

    def dispatch(i):
        q = quad(i)
        for e in range(4):
            j = q * 4 + e

            @pl.when(j != me)
            def _():
                s_copy(j, me).start()

            @pl.when(j == me)
            def _():
                recv[pl.ds(me * rb, rb), :] = send[pl.ds(me * rb, rb), :]

    def spread(k, p):
        if pair:
            w_copy(k, p, 4, me).start()
        w_copy(k, p, 3, core).start()

    def from_mid(k):
        for p in mine:
            w_copy(k, p, 2, me).wait_recv()
            spread(k, p)

    @pl.loop(1, outer + 1)
    def _(s):
        for p in mine:

            @pl.when(o - s >= 0)
            def _():
                k = idx(o - s, m, c)
                w_copy(k, p, 0, me).wait_recv()

                @pl.when(o + 1 < outer)
                def _():
                    w_copy(k, p, 0, up_dest()).start()

                w_copy(k, p, 2, mid).start()
                spread(k, p)

            @pl.when(o + s < outer)
            def _():
                k = idx(o + s, m, c)
                w_copy(k, p, 1, me).wait_recv()

                @pl.when(o > 0)
                def _():
                    w_copy(k, p, 1, down_dest()).start()

                w_copy(k, p, 2, mid).start()
                spread(k, p)

        t = s - 1

        @pl.when(o - t >= 0)
        def _():
            from_mid(idx(o - t, 1 - m, c))

        @pl.when((t > 0) & (o + t < outer))
        def _():
            from_mid(idx(o + t, 1 - m, c))

        @pl.when(s == 1)
        def _():
            @pl.loop(1, outer + 1)
            def _(i):
                dispatch(i)

    rank = rank_ref[0]
    scale = 32.0 / jnp.full((1, 128), rank, jnp.int32).astype(F32)
    lane = lax.broadcasted_iota(jnp.int32, (1, 128), 1)
    mask = jnp.where(lax.rem(lane, rank_max) < rank, 1.0, 0.0)
    lane_chunk = lax.broadcasted_iota(jnp.int32, (gb, lanes), 1) // rank_max
    diag = lane_chunk == chunk_ref[...]
    fold = jnp.where(foldc_ref[...] == foldr_ref[...], 1.0, 0.0).astype(BF16)
    half = lax.broadcasted_iota(jnp.int32, (gb, 128), 1) < rank_max

    def narrow(y):
        y = jnp.where(diag, y, 0.0)
        z = y[:, :128]
        for k in range(1, lanes // 128):
            z = z + y[:, k * 128 : (k + 1) * 128]
        z = z + pltpu.roll(z, rank_max, 1)
        hi = z.astype(BF16).astype(F32)
        return jnp.where(half, hi, z - hi).astype(BF16)

    def widen(z):
        return jnp.where(diag, jnp.concatenate([z] * (lanes // 128), axis=1), 0.0).astype(BF16)

    @pl.loop(1, outer + 1)
    def _(i):
        q = lax.rem(o + outer - i, outer)
        for e in range(4):
            j = q * 4 + e

            @pl.when(j != me)
            def _():
                s_copy(j, j).wait_recv()

        at = pl.ds(q * gb, gb)
        low = narrow(dot(recv[at, :xw], acat[...], 1, 1))
        lg = narrow(dot(recv[at, xw:], upst[...], 1, 1))
        both = dot(fold, jnp.concatenate([low, lg], axis=1))
        low = both[:, :128]
        lg = both[:, 128:]
        low = ((low + pltpu.roll(low, rank_max, 1)) * mask).astype(BF16).astype(F32)
        lg = ((lg + pltpu.roll(lg, rank_max, 1)) * (scale * mask)).astype(BF16).astype(F32)
        low = widen(low)
        lg = widen(lg)
        lowx[at, :] = low
        lgx[at, :] = lg
        ret[at, :xw] = dot(lg, acat[...]).astype(BF16)
        ret[at, xw:] = (dot(low, upst[...]) * scale[:, :1]).astype(BF16)
        for e in range(4):
            j = q * 4 + e

            @pl.when(j != me)
            def _():
                r_copy(j, me).start()

            @pl.when(j == me)
            def _():
                back[pl.ds(me * rb, rb), :] = ret[pl.ds(me * rb, rb), :]

    du = dot(lowx[...], recv[:, xw:], 0, 0) * scale[:, :1]
    for k in range(CHUNKS):
        du_ref[:, k * gw : (k + 1) * gw] = du[k * rank_max : (k + 1) * rank_max, :]

    for k in range(xw // 256):
        da = dot(lgx[...], recv[:, k * 256 : (k + 1) * 256], 0, 0)
        for e in range(CHUNKS):
            at = e * xw + k * 256
            da_ref[:, at : at + 256] = da[e * rank_max : (e + 1) * rank_max, :]

    def take(k):
        for p in theirs:
            w_copy(k, p, 4, me).wait_recv()
            w_copy(k, p, 3, core).start()

    @pl.loop(1, outer + 1)
    def _(s):
        for mm, t in ((m, s), (1 - m, s - 1)):

            @pl.when(o - t >= 0)
            def _():
                take(idx(o - t, mm, c))

            @pl.when((t > 0) & (o + t < outer))
            def _():
                take(idx(o + t, mm, c))

    vacc[...] = jnp.zeros_like(vacc)
    gacc[:, xw:] = jnp.zeros((CHUNKS * tl, gw), F32)

    def product(k):
        cols = pl.ds(pl.multiple_of(k * rows, rows), rows)
        vacc[...] += dot(tok_ref[:, cols], wbuf[k])
        at = pl.ds(pl.multiple_of(k * rows // xw * tl, tl), tl)
        part = pl.ds(pl.multiple_of(lax.rem(k * rows, xw), rows), rows)
        gacc[at, part] = dot(g_ref[...], wbuf[k], 1, 1)

    @pl.loop(0, n // 2)
    def _(k):
        product(2 * k + c)

    @pl.loop(0, n // 2)
    def _(k):
        s = 2 * k + 1 - c
        for p in range(PIECES):
            w_copy(s, p, 3, me).wait_recv()
        product(s)

    slot_key = jnp.concatenate([slot_c + k * slots for k in range(CHUNKS)], axis=0)

    @pl.loop(1, outer + 1)
    def _(i):
        q = quad(i)
        for e in range(4):
            j = q * 4 + e

            @pl.when(j != me)
            def _():
                r_copy(j, j).wait_recv()

        sel = jnp.where(slot_key == keyr_ref[...] + q * (4 * cap), 1.0, 0.0).astype(BF16)
        gacc[...] += dot(sel, back[pl.ds(q * gb, gb), :])

    for k in range(CHUNKS):
        at = slice(k * tl, (k + 1) * tl)
        gin_ref[:, k * xw : (k + 1) * xw] = gacc[at, :xw].astype(BF16)
        vcols = slice(k * gw, (k + 1) * gw)
        val_ref[:, vcols] = (vacc[:, vcols] + gacc[at, xw:]).astype(BF16)

    @pl.loop(0, n)
    def _(j):
        @pl.when(j != me)
        def _():
            s_copy(j, me).wait_send()
            r_copy(j, me).wait_send()

    @pl.loop(0, outer)
    def _(z):
        k = idx(z, m, c)
        far = idx(z, 1 - m, c)
        for p in mine:

            @pl.when((z <= o) & (o + 1 < outer))
            def _():
                w_copy(k, p, 0, up_dest()).wait_send()

            @pl.when((z >= o) & (o > 0))
            def _():
                w_copy(k, p, 1, down_dest()).wait_send()

            w_copy(k, p, 2, mid).wait_send()
            if pair:

                @pl.when(z != o)
                def _():
                    w_copy(k, p, 4, me).wait_send()

                w_copy(far, p, 4, me).wait_send()
        for p in range(PIECES):
            w_copy(k, p, 3, core).wait_send()
            w_copy(far, p, 3, core).wait_send()


def shards(tokens, job, weight, gradient, down, up, rank):
    n = lax.axis_size("fsdp")
    tl, width = tokens.shape
    wide = gradient.shape[1]
    rank_max = up.shape[1]
    cap = 5 * tl // (4 * n)
    rb = CHUNKS * cap
    gb = 4 * rb
    total = n * rb
    xw, gw = width // CHUNKS, wide // CHUNKS
    lanes = CHUNKS * rank_max

    i = np.arange(total)
    key = (i % rb // cap) * (n * cap) + (i // rb) * cap + i % cap
    fold = (i // rb) * cap + i % cap
    consts = [
        key[:gb, None],
        key[None, :gb],
        fold[:gb, None],
        fold[None, :gb],
        (i % rb // cap)[:gb, None],
    ]
    consts = [jnp.asarray(v, jnp.int32) for v in consts]

    vmem = pl.BlockSpec(memory_space=pltpu.VMEM)
    args = (rank, job, job.reshape(1, tl), *consts, tokens, gradient, weight, down[0].T, up[0])
    specs = [pl.BlockSpec(memory_space=pltpu.SMEM)] + [vmem] * 9
    specs += [pl.BlockSpec(memory_space=pl.ANY)] + [vmem] * 2
    dma = pltpu.SemaphoreType.DMA
    values, grad_in, d_down, d_up = pl.pallas_call(
        functools.partial(kernel, n, cap),
        out_shape=(
            jax.ShapeDtypeStruct((tl, wide), BF16),
            jax.ShapeDtypeStruct((tl, width), BF16),
            jax.ShapeDtypeStruct((rank_max, width), F32),
            jax.ShapeDtypeStruct((rank_max, wide), F32),
        ),
        in_specs=specs,
        out_specs=(vmem,) * 4,
        scratch_shapes=[
            pltpu.VMEM((n, *weight.shape), BF16),
            pltpu.VMEM((CHUNKS * tl, xw + gw), BF16),
            pltpu.VMEM((total, xw + gw), BF16),
            pltpu.VMEM((total, xw + gw), BF16),
            pltpu.VMEM((total, xw + gw), BF16),
            pltpu.VMEM((total, xw + gw), BF16),
            pltpu.VMEM((lanes, xw), BF16),
            pltpu.VMEM((lanes, gw), BF16),
            pltpu.VMEM((total, lanes), BF16),
            pltpu.VMEM((total, lanes), BF16),
            pltpu.VMEM((CHUNKS * tl, xw + gw), F32),
            pltpu.VMEM((tl, wide), F32),
            dma,
            dma((5, n, PIECES)),
            dma((n, PIECES)),
            dma((n,)),
            dma((n,)),
            dma((n,)),
            dma((n,)),
        ],
        compiler_params=pltpu.CompilerParams(
            collective_id=0, has_side_effects=True, vmem_limit_bytes=62 * 1024 * 1024
        ),
        cost_estimate=pl.CostEstimate(
            flops=16 * 10**9, bytes_accessed=16 * 2**20, transcendentals=0
        ),
    )(*args)
    return values, grad_in, d_down.T[None], d_up[None]


def solution(mesh):
    rows = P(("groups", "fsdp"), None)
    jobs = P(("groups", "fsdp"), None, None)
    return jax.shard_map(
        shards,
        mesh=mesh,
        in_specs=(rows, rows, P("fsdp", None), rows, jobs, jobs, P(("groups", "fsdp"))),
        out_specs=(rows, rows, jobs, jobs),
        check_vma=False,
    )
```

```python
import functools

import jax
import jax.numpy as jnp
import numpy as np
from jax import lax
from jax.experimental import pallas as pl
from jax.experimental.pallas import tpu as pltpu
from jax.sharding import PartitionSpec as P

CHUNKS = 8
PIECES = 4
BF16 = jnp.bfloat16
F32 = jnp.float32
MESH = pl.DeviceIdType.MESH


def dot(a, b, ca=1, cb=0):
    return lax.dot_general(a, b, (((ca,), (cb,)), ((), ())), preferred_element_type=F32)


def kernel(
    n,
    cap,
    rank_ref,
    jobr_ref,
    keyc_ref,
    keyr_ref,
    foldc_ref,
    foldr_ref,
    chunk_ref,
    tok_ref,
    g_ref,
    w_ref,
    a_ref,
    up_ref,
    val_ref,
    gin_ref,
    da_ref,
    du_ref,
    wbuf,
    stack,
    send,
    recv,
    ret,
    back,
    acat,
    upst,
    lowx,
    lgx,
    gacc,
    vacc,
    wl_sem,
    w_send,
    w_recv,
    s_send,
    s_recv,
    r_send,
    r_recv,
):
    me = lax.axis_index("fsdp")
    rb = CHUNKS * cap
    gb = 4 * rb
    outer = n // 4
    slots = n * cap
    tl, width = tok_ref.shape
    wide = g_ref.shape[1]
    xw = width // CHUNKS
    gw = wide // CHUNKS
    rank_max = up_ref.shape[0]
    lanes = CHUNKS * rank_max
    rows = wbuf.shape[1]
    prow = rows // PIECES
    o, m, c = me // 4, lax.rem(me // 2, 2), lax.rem(me, 2)

    def idx(oo, mm, cc):
        return (oo * 2 + mm) * 2 + cc

    local = pltpu.make_async_copy(w_ref, wbuf.at[me], wl_sem)
    local.start()

    barrier = pltpu.get_barrier_semaphore()

    @pl.loop(1, n)
    def _(d):
        pl.semaphore_signal(
            barrier, inc=1, device_id={"fsdp": lax.rem(me + d, n)}, device_id_type=MESH
        )

    pair = lax.axis_size("groups") % 2 == 0
    group = lax.axis_index("groups")
    other = group + 1 - 2 * lax.rem(group, 2) if pair else group
    mine = [lax.rem(group, 2) * 2 + v for v in range(2)] if pair else list(range(PIECES))
    theirs = [2 - lax.rem(group, 2) * 2 + v for v in range(2)] if pair else []

    if pair:
        pl.semaphore_signal(
            barrier, inc=1, device_id={"groups": other, "fsdp": me}, device_id_type=MESH
        )
    pl.semaphore_wait(barrier, n if pair else n - 1)
    local.wait()

    def w_copy(shard, piece, kind, dest):
        part = wbuf.at[shard, pl.ds(pl.multiple_of(piece * prow, prow), prow)]
        return pltpu.make_async_remote_copy(
            src_ref=part,
            dst_ref=part,
            send_sem=w_send.at[kind, shard, piece],
            recv_sem=w_recv.at[shard, piece],
            device_id={"groups": other if kind == 4 else group, "fsdp": dest},
            device_id_type=MESH,
        )

    def up_dest():
        return lax.rem(me + 4, n)

    def down_dest():
        return lax.rem(me + n - 4, n)

    mid = idx(o, 1 - m, c)
    core = idx(o, m, 1 - c)

    for p in mine:

        @pl.when(o + 1 < outer)
        def _():
            w_copy(me, p, 0, up_dest()).start()

        @pl.when(o > 0)
        def _():
            w_copy(me, p, 1, down_dest()).start()

    for p in mine:
        w_copy(me, p, 2, mid).start()
    for p in range(PIECES):
        w_copy(me, p, 3, core).start()

    jr = jobr_ref[...]
    ri = lax.broadcasted_iota(jnp.int32, (tl, tl), 0)
    ci = lax.broadcasted_iota(jnp.int32, (tl, tl), 1)
    jc = jnp.sum(jnp.where(ri == ci, jr, 0).astype(F32), axis=1, keepdims=True).astype(jnp.int32)
    one = jnp.where(jc == jr, 1.0, 0.0)
    pos_c = jnp.sum(jnp.where(ci < ri, one, 0.0), axis=1, keepdims=True).astype(jnp.int32)
    pos_r = jnp.sum(jnp.where(ri < ci, one, 0.0), axis=0, keepdims=True).astype(jnp.int32)
    slot_c = jc * cap + pos_c
    slot_r = jr * cap + pos_r

    for k in range(CHUNKS):
        stack[k * tl : (k + 1) * tl, :xw] = tok_ref[:, k * xw : (k + 1) * xw]
        stack[k * tl : (k + 1) * tl, xw:] = g_ref[:, k * gw : (k + 1) * gw]
    tok_key = jnp.concatenate([slot_r + k * slots for k in range(CHUNKS)], axis=1)

    def s_copy(j, k):
        return pltpu.make_async_remote_copy(
            src_ref=send.at[pl.ds(j * rb, rb)],
            dst_ref=recv.at[pl.ds(k * rb, rb)],
            send_sem=s_send.at[j],
            recv_sem=s_recv.at[k],
            device_id={"fsdp": j},
            device_id_type=MESH,
        )

    def r_copy(j, k):
        return pltpu.make_async_remote_copy(
            src_ref=ret.at[pl.ds(j * rb, rb)],
            dst_ref=back.at[pl.ds(k * rb, rb)],
            send_sem=r_send.at[j],
            recv_sem=r_recv.at[k],
            device_id={"fsdp": j},
            device_id_type=MESH,
        )

    def quad(i):
        return lax.rem(o + i, outer)

    @pl.loop(1, outer + 1)
    def _(i):
        q = quad(i)
        key = keyc_ref[...] + q * (4 * cap)
        sel = jnp.where(key == tok_key, 1.0, 0.0).astype(BF16)
        send[pl.ds(q * gb, gb), :] = dot(sel, stack[...]).astype(BF16)

    for k in range(CHUNKS):
        acat[k * rank_max : (k + 1) * rank_max, :] = a_ref[:, k * xw : (k + 1) * xw]
        upst[k * rank_max : (k + 1) * rank_max, :] = up_ref[:, k * gw : (k + 1) * gw]

    def dispatch(i):
        q = quad(i)
        for e in range(4):
            j = q * 4 + e

            @pl.when(j != me)
            def _():
                s_copy(j, me).start()

            @pl.when(j == me)
            def _():
                recv[pl.ds(me * rb, rb), :] = send[pl.ds(me * rb, rb), :]

    def spread(k, p):
        if pair:
            w_copy(k, p, 4, me).start()
        w_copy(k, p, 3, core).start()

    def from_mid(k):
        for p in mine:
            w_copy(k, p, 2, me).wait_recv()
            spread(k, p)

    @pl.loop(1, outer + 1)
    def _(s):
        for p in mine:

            @pl.when(o - s >= 0)
            def _():
                k = idx(o - s, m, c)
                w_copy(k, p, 0, me).wait_recv()

                @pl.when(o + 1 < outer)
                def _():
                    w_copy(k, p, 0, up_dest()).start()

                w_copy(k, p, 2, mid).start()
                spread(k, p)

            @pl.when(o + s < outer)
            def _():
                k = idx(o + s, m, c)
                w_copy(k, p, 1, me).wait_recv()

                @pl.when(o > 0)
                def _():
                    w_copy(k, p, 1, down_dest()).start()

                w_copy(k, p, 2, mid).start()
                spread(k, p)

        t = s - 1

        @pl.when(o - t >= 0)
        def _():
            from_mid(idx(o - t, 1 - m, c))

        @pl.when((t > 0) & (o + t < outer))
        def _():
            from_mid(idx(o + t, 1 - m, c))

        @pl.when(s == 1)
        def _():
            @pl.loop(1, outer + 1)
            def _(i):
                dispatch(i)

    rank = rank_ref[0]
    scale = 32.0 / jnp.full((1, 128), rank, jnp.int32).astype(F32)
    lane = lax.broadcasted_iota(jnp.int32, (1, 128), 1)
    mask = jnp.where(lax.rem(lane, rank_max) < rank, 1.0, 0.0)
    lane_chunk = lax.broadcasted_iota(jnp.int32, (gb, lanes), 1) // rank_max
    diag = lane_chunk == chunk_ref[...]
    fold = jnp.where(foldc_ref[...] == foldr_ref[...], 1.0, 0.0).astype(BF16)
    half = lax.broadcasted_iota(jnp.int32, (gb, 128), 1) < rank_max

    def narrow(y):
        y = jnp.where(diag, y, 0.0)
        z = y[:, :128]
        for k in range(1, lanes // 128):
            z = z + y[:, k * 128 : (k + 1) * 128]
        z = z + pltpu.roll(z, rank_max, 1)
        hi = z.astype(BF16).astype(F32)
        return jnp.where(half, hi, z - hi).astype(BF16)

    def widen(z):
        return jnp.where(diag, jnp.concatenate([z] * (lanes // 128), axis=1), 0.0).astype(BF16)

    @pl.loop(1, outer + 1)
    def _(i):
        q = lax.rem(o + outer - i, outer)
        for e in range(4):
            j = q * 4 + e

            @pl.when(j != me)
            def _():
                s_copy(j, j).wait_recv()

        at = pl.ds(q * gb, gb)
        low = narrow(dot(recv[at, :xw], acat[...], 1, 1))
        lg = narrow(dot(recv[at, xw:], upst[...], 1, 1))
        both = dot(fold, jnp.concatenate([low, lg], axis=1))
        low = both[:, :128]
        lg = both[:, 128:]
        low = ((low + pltpu.roll(low, rank_max, 1)) * mask).astype(BF16).astype(F32)
        lg = ((lg + pltpu.roll(lg, rank_max, 1)) * (scale * mask)).astype(BF16).astype(F32)
        low = widen(low)
        lg = widen(lg)
        lowx[at, :] = low
        lgx[at, :] = lg
        ret[at, :xw] = dot(lg, acat[...]).astype(BF16)
        ret[at, xw:] = (dot(low, upst[...]) * scale[:, :1]).astype(BF16)
        for e in range(4):
            j = q * 4 + e

            @pl.when(j != me)
            def _():
                r_copy(j, me).start()

            @pl.when(j == me)
            def _():
                back[pl.ds(me * rb, rb), :] = ret[pl.ds(me * rb, rb), :]

    du = dot(lowx[...], recv[:, xw:], 0, 0) * scale[:, :1]
    for k in range(CHUNKS):
        du_ref[:, k * gw : (k + 1) * gw] = du[k * rank_max : (k + 1) * rank_max, :]

    for k in range(xw // 256):
        da = dot(lgx[...], recv[:, k * 256 : (k + 1) * 256], 0, 0)
        for e in range(CHUNKS):
            at = e * xw + k * 256
            da_ref[:, at : at + 256] = da[e * rank_max : (e + 1) * rank_max, :]

    def take(k):
        for p in theirs:
            w_copy(k, p, 4, me).wait_recv()
            w_copy(k, p, 3, core).start()

    @pl.loop(1, outer + 1)
    def _(s):
        for mm, t in ((m, s), (1 - m, s - 1)):

            @pl.when(o - t >= 0)
            def _():
                take(idx(o - t, mm, c))

            @pl.when((t > 0) & (o + t < outer))
            def _():
                take(idx(o + t, mm, c))

    vacc[...] = jnp.zeros_like(vacc)
    gacc[:, xw:] = jnp.zeros((CHUNKS * tl, gw), F32)

    def product(k):
        cols = pl.ds(pl.multiple_of(k * rows, rows), rows)
        vacc[...] += dot(tok_ref[:, cols], wbuf[k])
        at = pl.ds(pl.multiple_of(k * rows // xw * tl, tl), tl)
        part = pl.ds(pl.multiple_of(lax.rem(k * rows, xw), rows), rows)
        gacc[at, part] = dot(g_ref[...], wbuf[k], 1, 1)

    @pl.loop(0, n // 2)
    def _(k):
        product(2 * k + c)

    @pl.loop(0, n // 2)
    def _(k):
        s = 2 * k + 1 - c
        for p in range(PIECES):
            w_copy(s, p, 3, me).wait_recv()
        product(s)

    slot_key = jnp.concatenate([slot_c + k * slots for k in range(CHUNKS)], axis=0)

    @pl.loop(1, outer + 1)
    def _(i):
        q = quad(i)
        for e in range(4):
            j = q * 4 + e

            @pl.when(j != me)
            def _():
                r_copy(j, j).wait_recv()

        sel = jnp.where(slot_key == keyr_ref[...] + q * (4 * cap), 1.0, 0.0).astype(BF16)
        gacc[...] += dot(sel, back[pl.ds(q * gb, gb), :])

    for k in range(CHUNKS):
        at = slice(k * tl, (k + 1) * tl)
        gin_ref[:, k * xw : (k + 1) * xw] = gacc[at, :xw].astype(BF16)
        vcols = slice(k * gw, (k + 1) * gw)
        val_ref[:, vcols] = (vacc[:, vcols] + gacc[at, xw:]).astype(BF16)

    @pl.loop(0, n)
    def _(j):
        @pl.when(j != me)
        def _():
            s_copy(j, me).wait_send()
            r_copy(j, me).wait_send()

    @pl.loop(0, outer)
    def _(z):
        k = idx(z, m, c)
        far = idx(z, 1 - m, c)
        for p in mine:

            @pl.when((z <= o) & (o + 1 < outer))
            def _():
                w_copy(k, p, 0, up_dest()).wait_send()

            @pl.when((z >= o) & (o > 0))
            def _():
                w_copy(k, p, 1, down_dest()).wait_send()

            w_copy(k, p, 2, mid).wait_send()
            if pair:

                @pl.when(z != o)
                def _():
                    w_copy(k, p, 4, me).wait_send()

                w_copy(far, p, 4, me).wait_send()
        for p in range(PIECES):
            w_copy(k, p, 3, core).wait_send()
            w_copy(far, p, 3, core).wait_send()


def shards(tokens, job, weight, gradient, down, up, rank):
    n = lax.axis_size("fsdp")
    tl, width = tokens.shape
    wide = gradient.shape[1]
    rank_max = up.shape[1]
    cap = 5 * tl // (4 * n)
    rb = CHUNKS * cap
    gb = 4 * rb
    total = n * rb
    xw, gw = width // CHUNKS, wide // CHUNKS
    lanes = CHUNKS * rank_max

    i = np.arange(total)
    key = (i % rb // cap) * (n * cap) + (i // rb) * cap + i % cap
    fold = (i // rb) * cap + i % cap
    consts = [
        key[:gb, None],
        key[None, :gb],
        fold[:gb, None],
        fold[None, :gb],
        (i % rb // cap)[:gb, None],
    ]
    consts = [jnp.asarray(v, jnp.int32) for v in consts]

    vmem = pl.BlockSpec(memory_space=pltpu.VMEM)
    args = (rank, job.reshape(1, tl), *consts, tokens, gradient, weight, down[0].T, up[0])
    specs = [pl.BlockSpec(memory_space=pltpu.SMEM)] + [vmem] * 8
    specs += [pl.BlockSpec(memory_space=pl.ANY)] + [vmem] * 2
    dma = pltpu.SemaphoreType.DMA
    values, grad_in, d_down, d_up = pl.pallas_call(
        functools.partial(kernel, n, cap),
        out_shape=(
            jax.ShapeDtypeStruct((tl, wide), BF16),
            jax.ShapeDtypeStruct((tl, width), BF16),
            jax.ShapeDtypeStruct((rank_max, width), F32),
            jax.ShapeDtypeStruct((rank_max, wide), F32),
        ),
        in_specs=specs,
        out_specs=(vmem,) * 4,
        scratch_shapes=[
            pltpu.VMEM((n, *weight.shape), BF16),
            pltpu.VMEM((CHUNKS * tl, xw + gw), BF16),
            pltpu.VMEM((total, xw + gw), BF16),
            pltpu.VMEM((total, xw + gw), BF16),
            pltpu.VMEM((total, xw + gw), BF16),
            pltpu.VMEM((total, xw + gw), BF16),
            pltpu.VMEM((lanes, xw), BF16),
            pltpu.VMEM((lanes, gw), BF16),
            pltpu.VMEM((total, lanes), BF16),
            pltpu.VMEM((total, lanes), BF16),
            pltpu.VMEM((CHUNKS * tl, xw + gw), F32),
            pltpu.VMEM((tl, wide), F32),
            dma,
            dma((5, n, PIECES)),
            dma((n, PIECES)),
            dma((n,)),
            dma((n,)),
            dma((n,)),
            dma((n,)),
        ],
        compiler_params=pltpu.CompilerParams(
            collective_id=0, has_side_effects=True, vmem_limit_bytes=62 * 1024 * 1024
        ),
        cost_estimate=pl.CostEstimate(
            flops=16 * 10**9, bytes_accessed=16 * 2**20, transcendentals=0
        ),
    )(*args)
    return values, grad_in, d_down.T[None], d_up[None]


def solution(mesh):
    rows = P(("groups", "fsdp"), None)
    jobs = P(("groups", "fsdp"), None, None)
    return jax.shard_map(
        shards,
        mesh=mesh,
        in_specs=(rows, rows, P("fsdp", None), rows, jobs, jobs, P(("groups", "fsdp"))),
        out_specs=(rows, rows, jobs, jobs),
        check_vma=False,
    )
```
